256 devices in a mesh: parent: 4 (over x_lo, core), child: 4 (over y), tile: 16 (over z, x_hi).
Axes of the slice: x: 4 (x_hi: 2, x_lo: 2; x = x_hi * 2 + x_lo), y: 4, z: 8, core: 2. Of those that a mesh axis runs over, the one named last changes fastest.
Arguments:
- children: float32 [16, 4, 512, 2048], P(('parent', 'child'), None, 'tile'), parts along dimension 0, as said below
Outputs:
- parent_map: float32 [16, 2, 512, 4, 1024], P('parent', None, 'tile', 'child'), parts along dimension 0
There are 4 independent parts, one for each index of `parent`. The reference program is written for one: setup_inputs(seed, part) draws one part's arguments, and reference() takes and returns one part's arrays. A program takes and returns all parts, laid end to end along the dimension named above; each array names one. Nothing has to cross between parts.
Inputs may be any that keep to these rules, and one draw needn't show every extreme that they name: `children`: each child's map, read as a matrix of order 4 * 512 in edge-major order, is exactly symmetric and has smallest eigenvalue 0.2 or more.
All inputs are finite; a program needn't handle non-finite values.
Results may differ from the reference program's by a relative error of at most 0.000088.
Values sent between devices are 32-bit elements; how exact they have to be, the bound alone decides.
No kernel may reach another device: no remote copies, remote signals or barrier semaphores. Data moves between devices by JAX's collectives and lax.ppermute only.
A program may use at most 128 MiB of HBM per device.

```python
import math
import jax
import jax.numpy as jnp
from jax import lax

EDGE = 512


def draw_children(key, part):
    key = jax.random.fold_in(key, 11)
    order_len = 4 * EDGE
    rank_len = min(64, EDGE // 4)
    key_mix = jax.random.fold_in(key, 0)
    key_diag = jax.random.fold_in(key, 1)
    key_amp = jax.random.fold_in(key, 3)
    mixing = jax.random.normal(key_mix, (4, order_len, order_len), jnp.float32)
    shifts = jnp.exp(jax.random.uniform(key_diag, (4, order_len), jnp.float32, -1.3862944, 0.0))
    strength = 24.0
    gram = jnp.einsum('cik,cjk->cij', mixing, mixing, precision=lax.Precision.HIGHEST) * (2.0 / order_len)
    points = jnp.arange(EDGE, dtype=jnp.float32) + 0.5
    mode_index = jnp.arange(rank_len, dtype=jnp.float32)
    profile = jnp.cos(math.pi / EDGE * points[:, None] * mode_index[None, :]) * math.sqrt(2.0 / EDGE)
    edge_profile = jnp.tile(profile, (4, 1))
    mode_amps = jax.random.uniform(key_amp, (4, rank_len), jnp.float32, 0.8, 1.25)
    weighted = edge_profile[None, :, :] * mode_amps[:, None, :]
    coherent = jnp.einsum('cik,jk->cij', weighted, edge_profile, precision=lax.Precision.HIGHEST) * strength
    identity = jnp.eye(order_len, dtype=jnp.float32)
    maps = gram + coherent
    maps = 0.5 * (maps + jnp.swapaxes(maps, 1, 2))
    maps = maps + identity[None, :, :] * shifts[:, :, None]
    return maps.reshape(4, 4, EDGE, order_len)


def setup_inputs(seed: int = 0, part: int = 0) -> dict:
    splits = jax.random.split(jax.random.key(seed), 2)
    own_keys = jax.random.split(jax.random.fold_in(splits[1], part), 2)
    children = draw_children(jax.random.fold_in(jax.random.fold_in(splits[1], part), 71), part)
    return {"children": children}


precise = lax.Precision.HIGHEST

def product_high(left_mat, right_mat):
    return jnp.dot(left_mat.astype(jnp.float32), right_mat.astype(jnp.float32), precision=precise, preferred_element_type=jnp.float32)

def lower_solve(factor, rhs_block):
    return jax.scipy.linalg.solve_triangular(factor, rhs_block, lower=True)

def reference(children):
    edge_len = EDGE

    def block(box, row_edge, col_edge):
        return children[box % 4, row_edge, :, col_edge * edge_len:(col_edge + 1) * edge_len]
    diagonal = [block(j, 0, 0) + block(j + 1, 1, 1) for j in range(4)]
    factor_zero = jnp.linalg.cholesky(diagonal[0])
    factor_two = jnp.linalg.cholesky(diagonal[2])
    couple_zero = jnp.concatenate([block(1, 1, 0), block(0, 0, 1)], axis=1)
    couple_two = jnp.concatenate([block(2, 0, 1), block(3, 1, 0)], axis=1)
    reach_zero = lower_solve(factor_zero, couple_zero)
    reach_two = lower_solve(factor_two, couple_two)
    zero_block = jnp.zeros((edge_len, edge_len), jnp.float32)
    odd_diag = jnp.concatenate([jnp.concatenate([diagonal[1], zero_block], axis=1), jnp.concatenate([zero_block, diagonal[3]], axis=1)], axis=0)
    reduced = odd_diag - product_high(reach_zero.T, reach_zero) - product_high(reach_two.T, reach_two)
    factor_odd = jnp.linalg.cholesky(reduced)

    def coupling(j):
        pieces = []
        for box in range(4):
            if box == j:
                pieces.append(children[box, 0, :, 2 * edge_len:])
            elif box == (j + 1) % 4:
                pieces.append(children[box, 1, :, 2 * edge_len:])
            else:
                pieces.append(jnp.zeros((edge_len, 2 * edge_len), jnp.float32))
        return jnp.concatenate(pieces, axis=1)
    lift_zero = lower_solve(factor_zero, coupling(0))
    lift_two = lower_solve(factor_two, coupling(2))
    odd_side = jnp.concatenate([coupling(1), coupling(3)], axis=0)
    odd_side = odd_side - product_high(reach_zero.T, lift_zero) - product_high(reach_two.T, lift_two)
    lift_odd = lower_solve(factor_odd, odd_side)
    lifted = jnp.concatenate([lift_zero, lift_two, lift_odd], axis=0)
    bound_diag = jnp.zeros((8 * edge_len, 8 * edge_len), jnp.float32)
    for box in range(4):
        own_block = children[box, 2:, :, 2 * edge_len:].reshape(2 * edge_len, 2 * edge_len)
        bound_diag = bound_diag.at[box * 2 * edge_len:(box + 1) * 2 * edge_len, box * 2 * edge_len:(box + 1) * 2 * edge_len].set(own_block)
    parent_map = bound_diag - product_high(lifted.T, lifted)
    return parent_map.reshape(4, 2, edge_len, 4, 2 * edge_len)
```

```python
import jax
import jax.numpy as jnp
from jax import lax
from jax.sharding import PartitionSpec as P

precise = lax.Precision.HIGHEST


def product_high(left_mat, right_mat):
    return jnp.dot(left_mat, right_mat, precision=precise, preferred_element_type=jnp.float32)


def factor_inverse(matrix):
    order_len = matrix.shape[0]
    if order_len <= 128:
        factor = jnp.linalg.cholesky(matrix)
        identity = jnp.eye(order_len, dtype=jnp.float32)
        return jax.scipy.linalg.solve_triangular(factor, identity, lower=True)
    half_len = order_len // 2
    inverse_top = factor_inverse(matrix[:half_len, :half_len])
    lower_left = product_high(matrix[half_len:, :half_len], inverse_top.T)
    schur_part = matrix[half_len:, half_len:] - product_high(lower_left, lower_left.T)
    inverse_bottom = factor_inverse(schur_part)
    inverse_left = -product_high(inverse_bottom, product_high(lower_left, inverse_top))
    upper_zero = jnp.zeros((half_len, order_len - half_len), jnp.float32)
    return jnp.concatenate(
        [
            jnp.concatenate([inverse_top, upper_zero], axis=1),
            jnp.concatenate([inverse_left, inverse_bottom], axis=1),
        ],
        axis=0,
    )


def inverse(matrix):
    lower = factor_inverse(matrix)
    return product_high(lower.T, lower)


def on_device(children):
    own = children[0]
    n = own.shape[2] // 4
    h = n // 2
    slab = own.shape[1]
    pos = lax.axis_index("child")
    is_even = pos % 2 == 0

    def halves(piece, keep_first):
        keep = jnp.where(keep_first, piece[:, :h], piece[:, h:])
        give = jnp.where(keep_first, piece[:, h:], piece[:, :h])
        return keep, give

    ev_keep, ev_give = halves(jnp.where(is_even, own[0, :, :n], own[1, :, n : 2 * n]), is_even)
    od_keep, od_give = halves(jnp.where(is_even, own[1, :, n : 2 * n], own[0, :, :n]), ~is_even)
    ev_slab = ev_keep + lax.ppermute(ev_give, "child", [(0, 1), (1, 0), (2, 3), (3, 2)])
    ev = lax.all_gather(ev_slab, ("child", "tile"), axis=0, tiled=True)
    couple = jnp.where(is_even, own[0, :, n : 2 * n], own[1, :, :n])
    cp = lax.all_gather(couple, ("child", "tile"), axis=0, tiled=True)
    od_slab = od_keep + lax.ppermute(od_give, "child", [(1, 2), (2, 1), (3, 0), (0, 3)])
    od = lax.all_gather(od_slab, ("child", "tile"), axis=0, tiled=True)
    points = own[2:, :, : 2 * n].reshape(2 * slab, 2 * n)
    b = lax.all_gather(points, "child", axis=0, tiled=False)
    cols0 = lax.all_gather(own[0, :, 2 * n :], "tile", axis=0, tiled=True)
    cols1 = lax.all_gather(own[1, :, 2 * n :], "tile", axis=0, tiled=True)

    ev = ev.reshape(4, n, h)
    cp = cp.reshape(4, n, n)
    od = od.reshape(4, n, h)
    inv0 = inverse(jnp.concatenate([ev[0], ev[1]], axis=1))
    inv2 = inverse(jnp.concatenate([ev[2], ev[3]], axis=1))
    c0 = jnp.concatenate([cp[1], cp[0]], axis=1)
    c2 = jnp.concatenate([cp[2], cp[3]], axis=1)
    k0 = product_high(inv0, c0)
    k2 = product_high(inv2, c2)
    zero = jnp.zeros((n, n), jnp.float32)
    odd = jnp.concatenate(
        [
            jnp.concatenate([od[1], od[2], zero], axis=1),
            jnp.concatenate([zero, od[3], od[0]], axis=1),
        ],
        axis=0,
    )
    inv_odd = inverse(odd - product_high(c0.T, k0) - product_high(c2.T, k2))

    be0 = jnp.concatenate([b[0][:, :n], b[1][:, n:]], axis=0)
    be2 = jnp.concatenate([b[2][:, :n], b[3][:, n:]], axis=0)
    z = jnp.zeros((2 * slab, n), jnp.float32)
    bo = jnp.concatenate(
        [
            jnp.concatenate([z, b[0][:, n:]], axis=1),
            jnp.concatenate([b[1][:, :n], z], axis=1),
            jnp.concatenate([b[2][:, n:], z], axis=1),
            jnp.concatenate([z, b[3][:, :n]], axis=1),
        ],
        axis=0,
    )
    yo = bo - jnp.concatenate([product_high(be0, k0), product_high(be2, k2)], axis=0)
    wo = product_high(yo, inv_odd)
    low_pair = pos < 2
    k_ev = jnp.where(low_pair, k0, k2)
    zz = jnp.zeros((4 * slab, n), jnp.float32)
    first = jnp.where(low_pair, product_high(be0, inv0), zz)
    second = jnp.where(low_pair, zz, product_high(be2, inv2))
    w_ev = jnp.concatenate([first, second], axis=0) - product_high(wo, k_ev.T)
    w_od = jnp.where((pos == 1) | (pos == 2), wo[:, :n], wo[:, n:])
    w0 = jnp.where(is_even, w_ev, w_od)
    w1 = jnp.where(is_even, w_od, w_ev)
    prod = product_high(w0, cols0) + product_high(w1, cols1)
    own_map = own[2:, :, 2 * n :]
    selector = (jnp.arange(4) == pos).astype(jnp.float32)
    res = selector[:, None, None, None] * own_map[None] - prod.reshape(4, 2, slab, 2 * n)
    return res.reshape(4, 2, slab, 1, 2 * n)


def solution(mesh):
    in_specs = (P(("parent", "child"), None, "tile", None),)
    out_specs = P("parent", None, "tile", "child", None)
    return jax.shard_map(
        on_device, mesh=mesh, in_specs=in_specs, out_specs=out_specs, check_vma=False
    )
```

```python
import jax
import jax.numpy as jnp
from jax import lax
from jax.experimental import pallas as pl
from jax.experimental.pallas import tpu as pltpu
from jax.sharding import PartitionSpec as P

precise = lax.Precision.HIGHEST
BLOCK = 128
GROUP = 8


def product_high(left_mat, right_mat):
    return jnp.dot(left_mat, right_mat, precision=precise, preferred_element_type=jnp.float32)


def product_left_t(left_mat, right_mat):
    return lax.dot_general(
        left_mat,
        right_mat,
        (((0,), (0,)), ((), ())),
        precision=precise,
        preferred_element_type=jnp.float32,
    )


def sweep_rows(groups, use_mxu):
    shape = (GROUP, BLOCK)
    sub = lax.broadcasted_iota(jnp.int32, shape, 0)
    lane = lax.broadcasted_iota(jnp.int32, shape, 1)

    def row_of(v, j):
        return jnp.broadcast_to(v[j : j + 1, :], shape)

    def col_of(v, j):
        return jnp.broadcast_to(v[:, j : j + 1], shape)

    top = groups[0]
    cols = [col_of(top, l) for l in range(GROUP)]
    for j in range(GROUP):
        pivot = 1.0 / row_of(cols[j], j)
        row = jnp.where(lane == j, pivot, row_of(top, j) * pivot)
        top = jnp.where(sub == j, row, jnp.where(lane == j, 0.0, top) - cols[j] * row)
        for l in range(j + 1, GROUP):
            entry = row_of(cols[l], j) * pivot
            cols[l] = jnp.where(sub == j, entry, cols[l] - cols[j] * entry)
    if use_mxu:
        rest = jnp.concatenate(groups[1:], axis=0)
        update = product_high(rest[:, :GROUP], top)
        lanes = lax.broadcasted_iota(jnp.int32, rest.shape, 1)
        rest = jnp.where(lanes < GROUP, 0.0, rest) - update
        return [top] + [rest[GROUP * h : GROUP * (h + 1)] for h in range(len(groups) - 1)]
    rows = [row_of(top, j) for j in range(GROUP)]
    out = [top]
    for v in groups[1:]:
        acc = jnp.where(lane < GROUP, 0.0, v)
        for j in range(GROUP):
            acc = acc - col_of(v, j) * rows[j]
        out.append(acc)
    return out


def invert_blocks(mats):
    count = BLOCK // GROUP
    use_mxu = len(mats) > 1

    def body(_, carry):
        out = []
        for i in range(len(mats)):
            groups = sweep_rows(list(carry[count * i : count * (i + 1)]), use_mxu)
            groups = [pltpu.roll(v, BLOCK - GROUP, 1) for v in groups]
            out += groups[1:] + groups[:1]
        return tuple(out)

    init = tuple(m[GROUP * h : GROUP * (h + 1), :] for m in mats for h in range(count))
    res = lax.fori_loop(0, count, body, init)
    return [jnp.concatenate(res[count * i : count * (i + 1)], axis=0) for i in range(len(mats))]


def even_kernel(ev_ref, inv_ref):
    n = inv_ref.shape[1]
    h = n // 2
    for i in range(2):
        for s in range(2):
            inv_ref[i, :, s * h : (s + 1) * h] = ev_ref[2 * i + s]
    for k in range(n // BLOCK):
        ks = slice(k * BLOCK, (k + 1) * BLOCK)
        diag = invert_blocks([inv_ref[i, ks, ks] for i in range(2)])
        for i in range(2):
            inv_ref[i, ks, ks] = jnp.eye(BLOCK, dtype=jnp.float32)
            row = product_high(diag[i], inv_ref[i, ks, :])
            for m in range(n // BLOCK):
                if m != k:
                    ms = slice(m * BLOCK, (m + 1) * BLOCK)
                    col = inv_ref[i, ms, ks]
                    inv_ref[i, ms, ks] = jnp.zeros((BLOCK, BLOCK), jnp.float32)
                    inv_ref[i, ms, :] = inv_ref[i, ms, :] - product_high(col, row)
            inv_ref[i, ks, :] = row


def even_inverses(ev):
    n = ev.shape[1]
    return pl.pallas_call(
        even_kernel,
        out_shape=jax.ShapeDtypeStruct((2, n, n), jnp.float32),
        compiler_params=pltpu.CompilerParams(vmem_limit_bytes=40 * 1024 * 1024),
        name="even_inverses",
    )(ev)


def odd_kernel(mat_in, rhs_in, mat_ref, rhs_ref):
    order = mat_in.shape[0]
    steps = order // BLOCK
    mat_ref[...] = mat_in[...]
    rhs_ref[...] = rhs_in[...]
    for k in range(steps):
        ks = slice(k * BLOCK, (k + 1) * BLOCK)
        rest = slice((k + 1) * BLOCK, order)
        (diag,) = invert_blocks([mat_ref[ks, ks]])
        if k + 1 < steps:
            mat_ref[ks, rest] = product_high(diag, mat_ref[ks, rest])
        rhs_ref[ks, :] = product_high(diag, rhs_ref[ks, :])

        def update(m, carry):
            @pl.when(m != k)
            def _():
                ms = pl.ds(pl.multiple_of(m * BLOCK, BLOCK), BLOCK)
                col = mat_ref[ms, ks]
                if k + 1 < steps:
                    mat_ref[ms, rest] = mat_ref[ms, rest] - product_high(col, mat_ref[ks, rest])
                rhs_ref[ms, :] = rhs_ref[ms, :] - product_high(col, rhs_ref[ks, :])

            return carry

        lax.fori_loop(0, steps, update, 0)


def odd_solve(mat, rhs):
    return pl.pallas_call(
        odd_kernel,
        out_shape=[
            jax.ShapeDtypeStruct(mat.shape, jnp.float32),
            jax.ShapeDtypeStruct(rhs.shape, jnp.float32),
        ],
        compiler_params=pltpu.CompilerParams(vmem_limit_bytes=40 * 1024 * 1024),
        name="odd_solve",
    )(mat, rhs)[1]


def on_device(children):
    own = children[0]
    n = own.shape[2] // 4
    h = n // 2
    slab = own.shape[1]
    pos = lax.axis_index("child")
    is_even = pos % 2 == 0

    def halves(piece, keep_first):
        keep = jnp.where(keep_first, piece[:, :h], piece[:, h:])
        give = jnp.where(keep_first, piece[:, h:], piece[:, :h])
        return keep, give

    ev_keep, ev_give = halves(jnp.where(is_even, own[0, :, :n], own[1, :, n : 2 * n]), is_even)
    od_keep, od_give = halves(jnp.where(is_even, own[1, :, n : 2 * n], own[0, :, :n]), ~is_even)
    ev_slab = ev_keep + lax.ppermute(ev_give, "child", [(0, 1), (1, 0), (2, 3), (3, 2)])
    ev = lax.all_gather(ev_slab, ("child", "tile"), axis=0, tiled=True)
    couple = jnp.where(is_even, own[0, :, n : 2 * n], own[1, :, :n])
    cp = lax.all_gather(couple, ("child", "tile"), axis=0, tiled=True)
    od_slab = od_keep + lax.ppermute(od_give, "child", [(1, 2), (2, 1), (3, 0), (0, 3)])
    od = lax.all_gather(od_slab, ("child", "tile"), axis=0, tiled=True)
    points = own[2:, :, : 2 * n].reshape(2 * slab, 2 * n)
    b = lax.all_gather(points, "child", axis=0, tiled=False)
    cols0 = lax.all_gather(own[0, :, 2 * n :], "tile", axis=0, tiled=True)
    cols1 = lax.all_gather(own[1, :, 2 * n :], "tile", axis=0, tiled=True)

    ev = ev.reshape(4, n, h)
    cp = cp.reshape(4, n, n)
    od = od.reshape(4, n, h)
    inverses = even_inverses(ev)
    inv0, inv2 = inverses[0], inverses[1]
    c0 = jnp.concatenate([cp[1], cp[0]], axis=1)
    c2 = jnp.concatenate([cp[2], cp[3]], axis=1)
    k0 = product_high(inv0, c0)
    k2 = product_high(inv2, c2)
    zero = jnp.zeros((n, n), jnp.float32)
    odd = jnp.concatenate(
        [
            jnp.concatenate([od[1], od[2], zero], axis=1),
            jnp.concatenate([zero, od[3], od[0]], axis=1),
        ],
        axis=0,
    )
    reduced = odd - product_left_t(c0, k0) - product_left_t(c2, k2)

    be0 = jnp.concatenate([b[0][:, :n], b[1][:, n:]], axis=0).T
    be2 = jnp.concatenate([b[2][:, :n], b[3][:, n:]], axis=0).T
    z = jnp.zeros((n, 2 * slab), jnp.float32)
    bo1 = jnp.concatenate([z, b[1][:, :n].T, b[2][:, n:].T, z], axis=1)
    bo3 = jnp.concatenate([b[0][:, n:].T, z, z, b[3][:, :n].T], axis=1)
    yo = jnp.concatenate([bo1, bo3], axis=0) - jnp.concatenate(
        [product_left_t(k0, be0), product_left_t(k2, be2)], axis=1
    )
    wo = odd_solve(reduced, yo)
    low_pair = pos < 2
    k_ev = jnp.where(low_pair, k0, k2)
    zz = jnp.zeros((n, 4 * slab), jnp.float32)
    first = jnp.where(low_pair, product_high(inv0, be0), zz)
    second = jnp.where(low_pair, zz, product_high(inv2, be2))
    w_ev = jnp.concatenate([first, second], axis=1) - product_high(k_ev, wo)
    w_od = jnp.where((pos == 1) | (pos == 2), wo[:n], wo[n:])
    w0 = jnp.where(is_even, w_ev, w_od)
    w1 = jnp.where(is_even, w_od, w_ev)
    prod = product_left_t(w0, cols0) + product_left_t(w1, cols1)
    own_map = own[2:, :, 2 * n :]
    selector = (jnp.arange(4) == pos).astype(jnp.float32)
    res = selector[:, None, None, None] * own_map[None] - prod.reshape(4, 2, slab, 2 * n)
    return res.reshape(4, 2, slab, 1, 2 * n)


def solution(mesh):
    in_specs = (P(("parent", "child"), None, "tile", None),)
    out_specs = P("parent", None, "tile", "child", None)
    return jax.shard_map(
        on_device, mesh=mesh, in_specs=in_specs, out_specs=out_specs, check_vma=False
    )
```

```python
import jax
import jax.numpy as jnp
from jax import lax
from jax.experimental import pallas as pl
from jax.experimental.pallas import tpu as pltpu
from jax.sharding import PartitionSpec as P

precise = lax.Precision.HIGHEST
BLOCK = 128
GROUP = 8


def product_high(left_mat, right_mat):
    return jnp.dot(left_mat, right_mat, precision=precise, preferred_element_type=jnp.float32)


def product_left_t(left_mat, right_mat):
    return lax.dot_general(
        left_mat,
        right_mat,
        (((0,), (0,)), ((), ())),
        precision=precise,
        preferred_element_type=jnp.float32,
    )


def sweep_rows(groups, use_mxu):
    shape = (GROUP, BLOCK)
    sub = lax.broadcasted_iota(jnp.int32, shape, 0)
    lane = lax.broadcasted_iota(jnp.int32, shape, 1)

    def row_of(v, j):
        return jnp.broadcast_to(v[j : j + 1, :], shape)

    def col_of(v, j):
        return jnp.broadcast_to(v[:, j : j + 1], shape)

    top = groups[0]
    cols = [col_of(top, l) for l in range(GROUP)]
    for j in range(GROUP):
        pivot = 1.0 / row_of(cols[j], j)
        row = jnp.where(lane == j, pivot, row_of(top, j) * pivot)
        top = jnp.where(sub == j, row, jnp.where(lane == j, 0.0, top) - cols[j] * row)
        for l in range(j + 1, GROUP):
            entry = row_of(cols[l], j) * pivot
            cols[l] = jnp.where(sub == j, entry, cols[l] - cols[j] * entry)
    if use_mxu:
        rest = jnp.concatenate(groups[1:], axis=0)
        update = product_high(rest[:, :GROUP], top)
        lanes = lax.broadcasted_iota(jnp.int32, rest.shape, 1)
        rest = jnp.where(lanes < GROUP, 0.0, rest) - update
        return [top] + [rest[GROUP * h : GROUP * (h + 1)] for h in range(len(groups) - 1)]
    rows = [row_of(top, j) for j in range(GROUP)]
    out = [top]
    for v in groups[1:]:
        acc = jnp.where(lane < GROUP, 0.0, v)
        for j in range(GROUP):
            acc = acc - col_of(v, j) * rows[j]
        out.append(acc)
    return out


def invert_blocks(mats):
    count = BLOCK // GROUP
    use_mxu = len(mats) > 1

    def body(_, carry):
        out = []
        for i in range(len(mats)):
            groups = sweep_rows(list(carry[count * i : count * (i + 1)]), use_mxu)
            groups = [pltpu.roll(v, BLOCK - GROUP, 1) for v in groups]
            out += groups[1:] + groups[:1]
        return tuple(out)

    init = tuple(m[GROUP * h : GROUP * (h + 1), :] for m in mats for h in range(count))
    res = lax.fori_loop(0, count, body, init)
    return [jnp.concatenate(res[count * i : count * (i + 1)], axis=0) for i in range(len(mats))]


def even_kernel(half_ref, own_ref, partner_ref, opposite_ref, mate_ref, inv_ref):
    n = inv_ref.shape[1]
    h = n // 2
    mine = pl.ds(pl.multiple_of(half_ref[0] * h, h), h)
    other = pl.ds(pl.multiple_of((1 - half_ref[0]) * h, h), h)
    inv_ref[0, :, mine] = own_ref[...]
    inv_ref[0, :, other] = partner_ref[...]
    inv_ref[1, :, mine] = opposite_ref[...]
    inv_ref[1, :, other] = mate_ref[...]
    for k in range(n // BLOCK):
        ks = slice(k * BLOCK, (k + 1) * BLOCK)
        diag = invert_blocks([inv_ref[i, ks, ks] for i in range(2)])
        for i in range(2):
            inv_ref[i, ks, ks] = jnp.eye(BLOCK, dtype=jnp.float32)
            row = product_high(diag[i], inv_ref[i, ks, :])
            for m in range(n // BLOCK):
                if m != k:
                    ms = slice(m * BLOCK, (m + 1) * BLOCK)
                    col = inv_ref[i, ms, ks]
                    inv_ref[i, ms, ks] = jnp.zeros((BLOCK, BLOCK), jnp.float32)
                    inv_ref[i, ms, :] = inv_ref[i, ms, :] - product_high(col, row)
            inv_ref[i, ks, :] = row


def even_inverses(half, pieces):
    n = pieces[0].shape[0]
    return pl.pallas_call(
        even_kernel,
        out_shape=jax.ShapeDtypeStruct((2, n, n), jnp.float32),
        in_specs=[pl.BlockSpec(memory_space=pltpu.SMEM)]
        + [pl.BlockSpec(memory_space=pltpu.VMEM)] * 4,
        out_specs=pl.BlockSpec(memory_space=pltpu.VMEM),
        compiler_params=pltpu.CompilerParams(vmem_limit_bytes=40 * 1024 * 1024),
        cost_estimate=pl.CostEstimate(flops=10**10, bytes_accessed=10**8, transcendentals=0),
        name="even_inverses",
    )(half, *pieces)


def odd_kernel(mat_in, rhs_in, mat_ref, rhs_ref):
    order = mat_in.shape[0]
    steps = order // BLOCK
    mat_ref[...] = mat_in[...]
    rhs_ref[...] = rhs_in[...]
    for k in range(steps):
        ks = slice(k * BLOCK, (k + 1) * BLOCK)
        rest = slice((k + 1) * BLOCK, order)
        (diag,) = invert_blocks([mat_ref[ks, ks]])
        if k + 1 < steps:
            mat_ref[ks, rest] = product_high(diag, mat_ref[ks, rest])
        rhs_ref[ks, :] = product_high(diag, rhs_ref[ks, :])

        def update(m, carry):
            @pl.when(m != k)
            def _():
                ms = pl.ds(pl.multiple_of(m * BLOCK, BLOCK), BLOCK)
                col = mat_ref[ms, ks]
                if k + 1 < steps:
                    mat_ref[ms, rest] = mat_ref[ms, rest] - product_high(col, mat_ref[ks, rest])
                rhs_ref[ms, :] = rhs_ref[ms, :] - product_high(col, rhs_ref[ks, :])

            return carry

        lax.fori_loop(0, steps, update, 0)


def odd_solve(mat, rhs):
    return pl.pallas_call(
        odd_kernel,
        out_shape=[
            jax.ShapeDtypeStruct(mat.shape, jnp.float32),
            jax.ShapeDtypeStruct(rhs.shape, jnp.float32),
        ],
        compiler_params=pltpu.CompilerParams(vmem_limit_bytes=40 * 1024 * 1024),
        cost_estimate=pl.CostEstimate(flops=10**10, bytes_accessed=10**8, transcendentals=0),
        name="odd_solve",
    )(mat, rhs)[1]


def siblings(piece):
    return [piece] + [
        lax.ppermute(piece, "child", [(i, i ^ x) for i in range(4)]) for x in range(1, 4)
    ]


def tiles(piece):
    count = lax.axis_size("tile")
    stack = jnp.broadcast_to(piece[None], (count,) + piece.shape)
    stack = lax.all_to_all(stack, "tile", 0, 0, tiled=False)
    return stack.reshape(count * piece.shape[0], piece.shape[1])


def by_relation(stack, pos):
    pick = [jnp.where(pos == 0, stack[i], 0.0) for i in range(4)]
    for x in range(1, 4):
        pick = [jnp.where(pos == x, stack[i ^ x], pick[i]) for i in range(4)]
    return jnp.stack(pick)


def on_device(children):
    own = children[0]
    n = own.shape[2] // 4
    h = n // 2
    slab = own.shape[1]
    pos = lax.axis_index("child")
    is_even = pos % 2 == 0

    def halves(piece, keep_first):
        keep = jnp.where(keep_first, piece[:, :h], piece[:, h:])
        give = jnp.where(keep_first, piece[:, h:], piece[:, :h])
        return keep, give

    ev_rows = jnp.where(is_even, own[0], own[1])
    od_rows = jnp.where(is_even, own[1], own[0])
    ev_diag = jnp.where(is_even, ev_rows[:, :n], ev_rows[:, n : 2 * n])
    od_diag = jnp.where(is_even, od_rows[:, n : 2 * n], od_rows[:, :n])
    couple = jnp.where(is_even, ev_rows[:, n : 2 * n], ev_rows[:, :n])
    points = own[2:, :, : 2 * n].reshape(2 * slab, 2 * n)
    points = jnp.where(is_even, points, jnp.concatenate([points[:, n:], points[:, :n]], axis=1))
    border = jnp.stack([ev_rows[:, 2 * n :], od_rows[:, 2 * n :]])
    ev_keep, ev_give = halves(ev_diag, is_even)
    od_keep, od_give = halves(od_diag, is_even)
    ev = ev_keep + lax.ppermute(ev_give, "child", [(i, i ^ 1) for i in range(4)])
    od = od_keep + lax.ppermute(od_give, "child", [(i, i ^ 3) for i in range(4)])
    b = lax.all_gather(points, "child", axis=0, tiled=False)
    ev = tiles(ev)
    ev, couple, border = lax.optimization_barrier((ev, couple, border))
    border = lax.all_gather(border, "tile", axis=0, tiled=True)
    ev = siblings(ev)
    cp = tiles(couple)
    cp, ev, od = lax.optimization_barrier((cp, ev, od))
    cp = siblings(cp)
    od = siblings(tiles(od))
    b = by_relation(b, pos)

    half = (pos % 2).astype(jnp.int32).reshape(1)
    inverses = even_inverses(half, ev)
    inv_own, inv_far = inverses[0], inverses[1]
    c_own = jnp.concatenate([cp[0], cp[1]], axis=1)
    c_far = jnp.concatenate([cp[3], cp[2]], axis=1)
    k_own = product_high(inv_own, c_own)
    k_far = product_high(inv_far, c_far)
    zero = jnp.zeros((n, n), jnp.float32)

    def joined(first, second):
        return jnp.where(
            is_even,
            jnp.concatenate([first, second], axis=1),
            jnp.concatenate([second, first], axis=1),
        )

    odd = jnp.concatenate(
        [
            jnp.concatenate([joined(od[0], od[3]), zero], axis=1),
            jnp.concatenate([zero, joined(od[2], od[1])], axis=1),
        ],
        axis=0,
    )
    reduced = odd - product_left_t(c_own, k_own) - product_left_t(c_far, k_far)

    be_own = jnp.concatenate([b[0][:, :n], b[1][:, :n]], axis=0).T
    be_far = jnp.concatenate([b[2][:, :n], b[3][:, :n]], axis=0).T
    z = jnp.zeros((n, 2 * slab), jnp.float32)
    bo_own = jnp.concatenate([b[0][:, n:].T, z, z, b[3][:, n:].T], axis=1)
    bo_far = jnp.concatenate([z, b[1][:, n:].T, b[2][:, n:].T, z], axis=1)
    yo = jnp.concatenate([bo_own, bo_far], axis=0) - jnp.concatenate(
        [product_left_t(k_own, be_own), product_left_t(k_far, be_far)], axis=1
    )
    wo = odd_solve(reduced, yo)
    we = jnp.concatenate(
        [product_high(inv_own, be_own), jnp.zeros((n, 4 * slab), jnp.float32)], axis=1
    ) - product_high(k_own, wo)
    w = jnp.stack([we, wo[:n]]).reshape(2, n // slab, slab, 8 * slab).transpose(1, 0, 2, 3)
    prod = product_left_t(w.reshape(2 * n, 8 * slab), border.reshape(2 * n, 2 * n))
    prod = prod.reshape(4, 2, slab, 2 * n)
    own_map = own[2:, :, 2 * n :]
    res = jnp.concatenate([(own_map - prod[0])[None], -prod[1:]], axis=0)
    return by_relation(res, pos).reshape(4, 2, slab, 1, 2 * n)


def solution(mesh):
    in_specs = (P(("parent", "child"), None, "tile", None),)
    out_specs = P("parent", None, "tile", "child", None)
    return jax.shard_map(
        on_device, mesh=mesh, in_specs=in_specs, out_specs=out_specs, check_vma=False
    )
```

```python
import jax
import jax.numpy as jnp
from jax import lax
from jax.experimental import pallas as pl
from jax.experimental.pallas import tpu as pltpu
from jax.sharding import PartitionSpec as P

precise = lax.Precision.HIGHEST
BLOCK = 128
GROUP = 8


def product_high(left_mat, right_mat):
    return jnp.dot(left_mat, right_mat, precision=precise, preferred_element_type=jnp.float32)


def product_left_t(left_mat, right_mat, precision=lax.Precision.HIGH):
    return lax.dot_general(
        left_mat,
        right_mat,
        (((0,), (0,)), ((), ())),
        precision=precision,
        preferred_element_type=jnp.float32,
    )


def split(mat):
    high = mat.astype(jnp.bfloat16)
    return high, (mat - high.astype(jnp.float32)).astype(jnp.bfloat16)


def wide_left(mat):
    high, low = split(mat)
    return jnp.concatenate([high, low, high], axis=1)


def wide_right(mat):
    high, low = split(mat)
    return jnp.concatenate([high, high, low], axis=0)


def product_wide(left_wide, right_wide):
    return jnp.dot(left_wide, right_wide, preferred_element_type=jnp.float32)


def pivot_group(rows, g):
    shape = (GROUP, BLOCK)
    sub = lax.broadcasted_iota(jnp.int32, shape, 0)
    lane = lax.broadcasted_iota(jnp.int32, shape, 1)
    first = GROUP * g

    def row_of(v, j):
        return jnp.broadcast_to(v[j : j + 1, :], shape)

    def col_of(v, j):
        return jnp.broadcast_to(v[:, first + j : first + j + 1], shape)

    top = rows[g]
    cols = [col_of(top, j) for j in range(GROUP)]
    pivot = row_of(cols[0], 0)
    for j in range(GROUP):
        inverse = 1.0 / pivot
        if j + 1 < GROUP:
            ahead = cols[j] * row_of(cols[j + 1], j)
            pivot = row_of(cols[j + 1], j + 1) - row_of(ahead, j + 1) * inverse
        scaled = jnp.where(lane == first + j, inverse, row_of(top, j) * inverse)
        cleared = jnp.where(lane == first + j, 0.0, top)
        top = jnp.where(sub == j, scaled, cleared - cols[j] * scaled)
        for l in range(j + 1, GROUP):
            entry = row_of(cols[l], j)
            cols[l] = jnp.where(sub == j, entry * inverse, cols[l] - (cols[j] * entry) * inverse)
    spread = [row_of(top, j) for j in range(GROUP)]
    out = []
    for h, v in enumerate(rows):
        if h == g:
            out.append(top)
            continue
        terms = [col_of(v, j) * spread[j] for j in range(GROUP)]
        while len(terms) > 1:
            terms = [terms[i] + terms[i + 1] for i in range(0, len(terms), 2)]
        pivots = (lane >= first) & (lane < first + GROUP)
        out.append(jnp.where(pivots, 0.0, v) - terms[0])
    return out


def invert_blocks(mats, width):
    count = BLOCK // GROUP
    inner = width // GROUP

    def body(_, carry):
        out = []
        for i in range(len(mats)):
            groups = list(carry[count * i : count * (i + 1)])
            panel = groups[:inner]
            for g in range(inner):
                panel = pivot_group(panel, g)
            panel = jnp.concatenate(panel, axis=0)
            rest = jnp.concatenate(groups[inner:], axis=0)
            update = product_high(rest[:, :width], panel)
            lanes = lax.broadcasted_iota(jnp.int32, rest.shape, 1)
            rest = jnp.where(lanes < width, 0.0, rest) - update
            turned = pltpu.roll(jnp.concatenate([rest, panel], axis=0), BLOCK - width, 1)
            out += [turned[GROUP * h : GROUP * (h + 1)] for h in range(count)]
        return tuple(out)

    init = tuple(m[GROUP * h : GROUP * (h + 1), :] for m in mats for h in range(count))
    res = lax.fori_loop(0, BLOCK // width, body, init)
    return [jnp.concatenate(res[count * i : count * (i + 1)], axis=0) for i in range(len(mats))]


def even_kernel(half_ref, own_ref, partner_ref, opposite_ref, mate_ref, inv_ref):
    n = inv_ref.shape[1]
    h = n // 2
    mine = pl.ds(pl.multiple_of(half_ref[0] * h, h), h)
    other = pl.ds(pl.multiple_of((1 - half_ref[0]) * h, h), h)
    inv_ref[0, :, mine] = own_ref[...]
    inv_ref[0, :, other] = partner_ref[...]
    inv_ref[1, :, mine] = opposite_ref[...]
    inv_ref[1, :, other] = mate_ref[...]
    for k in range(n // BLOCK):
        ks = slice(k * BLOCK, (k + 1) * BLOCK)
        diag = invert_blocks([inv_ref[i, ks, ks] for i in range(2)], 16)
        for i in range(2):
            inv_ref[i, ks, ks] = jnp.eye(BLOCK, dtype=jnp.float32)
            row = product_high(diag[i], inv_ref[i, ks, :])
            for m in range(n // BLOCK):
                if m != k:
                    ms = slice(m * BLOCK, (m + 1) * BLOCK)
                    col = inv_ref[i, ms, ks]
                    inv_ref[i, ms, ks] = jnp.zeros((BLOCK, BLOCK), jnp.float32)
                    inv_ref[i, ms, :] = inv_ref[i, ms, :] - product_high(col, row)
            inv_ref[i, ks, :] = row


def even_inverses(half, pieces):
    n = pieces[0].shape[0]
    return pl.pallas_call(
        even_kernel,
        out_shape=jax.ShapeDtypeStruct((2, n, n), jnp.float32),
        in_specs=[pl.BlockSpec(memory_space=pltpu.SMEM)]
        + [pl.BlockSpec(memory_space=pltpu.VMEM)] * 4,
        out_specs=pl.BlockSpec(memory_space=pltpu.VMEM),
        compiler_params=pltpu.CompilerParams(vmem_limit_bytes=40 * 1024 * 1024),
        cost_estimate=pl.CostEstimate(flops=10**10, bytes_accessed=10**8, transcendentals=0),
        name="even_inverses",
    )(half, *pieces)


def odd_kernel(mat_in, rhs_in, rhs_ref, mat_ref, row_ref):
    order = mat_in.shape[0]
    steps = order // BLOCK
    mat_ref[:, :order] = mat_in[...]
    mat_ref[:, order:] = rhs_in[...]
    diag = mat_in[:BLOCK, :BLOCK]
    for k in range(steps):
        ks = slice(k * BLOCK, (k + 1) * BLOCK)
        rest = slice((k + 1) * BLOCK, mat_ref.shape[1])
        (inverse,) = invert_blocks([diag], 64)
        row = product_wide(wide_left(inverse), wide_right(mat_ref[ks, rest]))
        row_ref[:, rest] = wide_right(row)
        if k + 1 < steps:
            nxt = slice((k + 1) * BLOCK, (k + 2) * BLOCK)
            diag = mat_ref[nxt, nxt] - product_wide(wide_left(mat_ref[nxt, ks]), row_ref[:, nxt])

        def update(m, carry):
            @pl.when(m != k)
            def _():
                ms = pl.ds(pl.multiple_of(m * BLOCK, BLOCK), BLOCK)
                col = wide_left(mat_ref[ms, ks])
                mat_ref[ms, rest] = mat_ref[ms, rest] - product_wide(col, row_ref[:, rest])

            return carry

        lax.fori_loop(0, steps, update, 0)
        mat_ref[ks, rest] = row
    rhs_ref[...] = mat_ref[:, order:]


def odd_solve(mat, rhs):
    order, count = rhs.shape
    return pl.pallas_call(
        odd_kernel,
        out_shape=jax.ShapeDtypeStruct(rhs.shape, jnp.float32),
        scratch_shapes=[
            pltpu.VMEM((order, order + count), jnp.float32),
            pltpu.VMEM((3 * BLOCK, order + count), jnp.bfloat16),
        ],
        compiler_params=pltpu.CompilerParams(vmem_limit_bytes=40 * 1024 * 1024),
        cost_estimate=pl.CostEstimate(flops=10**10, bytes_accessed=10**8, transcendentals=0),
        name="odd_solve",
    )(mat, rhs)


def siblings(piece):
    return [piece] + [
        lax.ppermute(piece, "child", [(i, i ^ x) for i in range(4)]) for x in range(1, 4)
    ]


def tiles(piece):
    count = lax.axis_size("tile")
    stack = jnp.broadcast_to(piece[None], (count,) + piece.shape)
    stack = lax.all_to_all(stack, "tile", 0, 0, tiled=False)
    return stack.reshape(count * piece.shape[0], piece.shape[1])


def by_relation(stack, pos):
    pick = [jnp.where(pos == 0, stack[i], 0.0) for i in range(4)]
    for x in range(1, 4):
        pick = [jnp.where(pos == x, stack[i ^ x], pick[i]) for i in range(4)]
    return jnp.stack(pick)


def on_device(children):
    own = children[0]
    n = own.shape[2] // 4
    h = n // 2
    slab = own.shape[1]
    pos = lax.axis_index("child")
    is_even = pos % 2 == 0

    def halves(piece, keep_first):
        keep = jnp.where(keep_first, piece[:, :h], piece[:, h:])
        give = jnp.where(keep_first, piece[:, h:], piece[:, :h])
        return keep, give

    ev_rows = jnp.where(is_even, own[0], own[1])
    od_rows = jnp.where(is_even, own[1], own[0])
    ev_diag = jnp.where(is_even, ev_rows[:, :n], ev_rows[:, n : 2 * n])
    od_diag = jnp.where(is_even, od_rows[:, n : 2 * n], od_rows[:, :n])
    couple = jnp.where(is_even, ev_rows[:, n : 2 * n], ev_rows[:, :n])
    points = own[2:, :, : 2 * n].reshape(2 * slab, 2 * n)
    points = jnp.where(is_even, points, jnp.concatenate([points[:, n:], points[:, :n]], axis=1))
    border = jnp.stack([ev_rows[:, 2 * n :], od_rows[:, 2 * n :]])
    ev_keep, ev_give = halves(ev_diag, is_even)
    od_keep, od_give = halves(od_diag, is_even)
    ev = ev_keep + lax.ppermute(ev_give, "child", [(i, i ^ 1) for i in range(4)])
    od = od_keep + lax.ppermute(od_give, "child", [(i, i ^ 3) for i in range(4)])
    b = lax.all_gather(points, "child", axis=0, tiled=False)
    ev = tiles(ev)
    ev, couple, border = lax.optimization_barrier((ev, couple, border))
    border = lax.all_gather(border, "tile", axis=0, tiled=True)
    ev = siblings(ev)
    cp = tiles(couple)
    cp, ev, od = lax.optimization_barrier((cp, ev, od))
    cp = siblings(cp)
    od = siblings(tiles(od))
    b = by_relation(b, pos)

    half = (pos % 2).astype(jnp.int32).reshape(1)
    inverses = even_inverses(half, ev)
    inv_own, inv_far = inverses[0], inverses[1]
    c_own = jnp.concatenate([cp[0], cp[1]], axis=1)
    c_far = jnp.concatenate([cp[3], cp[2]], axis=1)
    k_own = product_high(inv_own, c_own)
    k_far = product_high(inv_far, c_far)
    zero = jnp.zeros((n, n), jnp.float32)

    def joined(first, second):
        return jnp.where(
            is_even,
            jnp.concatenate([first, second], axis=1),
            jnp.concatenate([second, first], axis=1),
        )

    odd = jnp.concatenate(
        [
            jnp.concatenate([joined(od[0], od[3]), zero], axis=1),
            jnp.concatenate([zero, joined(od[2], od[1])], axis=1),
        ],
        axis=0,
    )
    reduced = odd - product_left_t(c_own, k_own) - product_left_t(c_far, k_far)

    be_own = jnp.concatenate([b[0][:, :n], b[1][:, :n]], axis=0).T
    be_far = jnp.concatenate([b[2][:, :n], b[3][:, :n]], axis=0).T
    z = jnp.zeros((n, 2 * slab), jnp.float32)
    bo_own = jnp.concatenate([b[0][:, n:].T, z, z, b[3][:, n:].T], axis=1)
    bo_far = jnp.concatenate([z, b[1][:, n:].T, b[2][:, n:].T, z], axis=1)
    yo = jnp.concatenate([bo_own, bo_far], axis=0) - jnp.concatenate(
        [product_left_t(k_own, be_own), product_left_t(k_far, be_far)], axis=1
    )
    wo = odd_solve(reduced, yo)
    we = jnp.concatenate(
        [product_high(inv_own, be_own), jnp.zeros((n, 4 * slab), jnp.float32)], axis=1
    ) - product_high(k_own, wo)
    w = jnp.stack([we, wo[:n]]).reshape(2, n // slab, slab, 8 * slab).transpose(1, 0, 2, 3)
    prod = product_left_t(w.reshape(2 * n, 8 * slab), border.reshape(2 * n, 2 * n))
    prod = prod.reshape(4, 2, slab, 2 * n)
    own_map = own[2:, :, 2 * n :]
    res = jnp.concatenate([(own_map - prod[0])[None], -prod[1:]], axis=0)
    return by_relation(res, pos).reshape(4, 2, slab, 1, 2 * n)


def solution(mesh):
    in_specs = (P(("parent", "child"), None, "tile", None),)
    out_specs = P("parent", None, "tile", "child", None)
    return jax.shard_map(
        on_device, mesh=mesh, in_specs=in_specs, out_specs=out_specs, check_vma=False
    )
```

```python
import jax
import jax.numpy as jnp
from jax import lax
from jax.experimental import pallas as pl
from jax.experimental.pallas import tpu as pltpu
from jax.sharding import PartitionSpec as P

precise = lax.Precision.HIGHEST
BLOCK = 128
GROUP = 8


def product_high(left_mat, right_mat):
    return jnp.dot(left_mat, right_mat, precision=precise, preferred_element_type=jnp.float32)


def product_left_t(left_mat, right_mat, precision=lax.Precision.HIGH):
    return lax.dot_general(
        left_mat,
        right_mat,
        (((0,), (0,)), ((), ())),
        precision=precision,
        preferred_element_type=jnp.float32,
    )


def split(mat):
    high = mat.astype(jnp.bfloat16)
    return high, (mat - high.astype(jnp.float32)).astype(jnp.bfloat16)


def wide_left(mat):
    high, low = split(mat)
    return jnp.concatenate([high, low, high], axis=1)


def wide_right(mat):
    high, low = split(mat)
    return jnp.concatenate([high, high, low], axis=0)


def product_wide(left_wide, right_wide):
    return jnp.dot(left_wide, right_wide, preferred_element_type=jnp.float32)


def pivot_group(rows, g):
    shape = (GROUP, BLOCK)
    sub = lax.broadcasted_iota(jnp.int32, shape, 0)
    lane = lax.broadcasted_iota(jnp.int32, shape, 1)
    first = GROUP * g

    def row_of(v, j):
        return jnp.broadcast_to(v[j : j + 1, :], shape)

    def col_of(v, j):
        return jnp.broadcast_to(v[:, first + j : first + j + 1], shape)

    top = rows[g]
    cols = [col_of(top, j) for j in range(GROUP)]
    pivot = row_of(cols[0], 0)
    for j in range(GROUP):
        inverse = 1.0 / pivot
        if j + 1 < GROUP:
            ahead = cols[j] * row_of(cols[j + 1], j)
            pivot = row_of(cols[j + 1], j + 1) - row_of(ahead, j + 1) * inverse
        scaled = jnp.where(lane == first + j, inverse, row_of(top, j) * inverse)
        cleared = jnp.where(lane == first + j, 0.0, top)
        top = jnp.where(sub == j, scaled, cleared - cols[j] * scaled)
        for l in range(j + 1, GROUP):
            entry = row_of(cols[l], j)
            cols[l] = jnp.where(sub == j, entry * inverse, cols[l] - (cols[j] * entry) * inverse)
    spread = [row_of(top, j) for j in range(GROUP)]
    out = []
    for h, v in enumerate(rows):
        if h == g:
            out.append(top)
            continue
        terms = [col_of(v, j) * spread[j] for j in range(GROUP)]
        while len(terms) > 1:
            terms = [terms[i] + terms[i + 1] for i in range(0, len(terms), 2)]
        pivots = (lane >= first) & (lane < first + GROUP)
        out.append(jnp.where(pivots, 0.0, v) - terms[0])
    return out


def invert_blocks(mats, width):
    count = BLOCK // GROUP
    inner = width // GROUP

    def body(_, carry):
        out = []
        for i in range(len(mats)):
            groups = list(carry[count * i : count * (i + 1)])
            panel = groups[:inner]
            for g in range(inner):
                panel = pivot_group(panel, g)
            panel = jnp.concatenate(panel, axis=0)
            rest = jnp.concatenate(groups[inner:], axis=0)
            update = product_high(rest[:, :width], panel)
            lanes = lax.broadcasted_iota(jnp.int32, rest.shape, 1)
            rest = jnp.where(lanes < width, 0.0, rest) - update
            turned = pltpu.roll(jnp.concatenate([rest, panel], axis=0), BLOCK - width, 1)
            out += [turned[GROUP * h : GROUP * (h + 1)] for h in range(count)]
        return tuple(out)

    init = tuple(m[GROUP * h : GROUP * (h + 1), :] for m in mats for h in range(count))
    res = lax.fori_loop(0, BLOCK // width, body, init)
    return [jnp.concatenate(res[count * i : count * (i + 1)], axis=0) for i in range(len(mats))]


def even_kernel(half_ref, mine_ref, other_ref, inv_ref):
    n = inv_ref.shape[0]
    h = n // 2
    mine = pl.ds(pl.multiple_of(half_ref[0] * h, h), h)
    other = pl.ds(pl.multiple_of((1 - half_ref[0]) * h, h), h)
    inv_ref[:, mine] = mine_ref[...]
    inv_ref[:, other] = other_ref[...]
    for k in range(n // BLOCK):
        ks = slice(k * BLOCK, (k + 1) * BLOCK)
        (diag,) = invert_blocks([inv_ref[ks, ks]], 64)
        inv_ref[ks, ks] = jnp.eye(BLOCK, dtype=jnp.float32)
        row = product_high(diag, inv_ref[ks, :])
        for m in range(n // BLOCK):
            if m != k:
                ms = slice(m * BLOCK, (m + 1) * BLOCK)
                col = inv_ref[ms, ks]
                inv_ref[ms, ks] = jnp.zeros((BLOCK, BLOCK), jnp.float32)
                inv_ref[ms, :] = inv_ref[ms, :] - product_high(col, row)
        inv_ref[ks, :] = row


def even_inverse(half, mine, other):
    n = mine.shape[0]
    return pl.pallas_call(
        even_kernel,
        out_shape=jax.ShapeDtypeStruct((n, n), jnp.float32),
        in_specs=[pl.BlockSpec(memory_space=pltpu.SMEM)]
        + [pl.BlockSpec(memory_space=pltpu.VMEM)] * 2,
        out_specs=pl.BlockSpec(memory_space=pltpu.VMEM),
        compiler_params=pltpu.CompilerParams(vmem_limit_bytes=40 * 1024 * 1024),
        cost_estimate=pl.CostEstimate(flops=10**10, bytes_accessed=10**8, transcendentals=0),
        name="even_inverse",
    )(half, mine, other)


def middle_kernel(
    inv_own, inv_far, c0, c1, c2, c3, b, k_own, corner, across, corner_far, near, away, w0, w1, w2, w3
):
    n = corner.shape[0]
    slab = b.shape[1]

    def chunk(m):
        return pl.ds(pl.multiple_of(m * BLOCK, BLOCK), BLOCK)

    for i, (inv, c, wide) in enumerate(
        ((inv_own, c0, w0), (inv_own, c1, w1), (inv_far, c3, w3), (inv_far, c2, w2))
    ):

        def solved(m, carry, i=i, inv=inv, c=c, wide=wide):
            rows = product_high(inv[chunk(m), :], c[...])
            if i < 2:
                k_own[chunk(m), i * n : (i + 1) * n] = rows
            high, low = split(rows)
            wide[0, chunk(m), :] = high
            wide[1, chunk(m), :] = high
            wide[2, chunk(m), :] = low
            return carry

        lax.fori_loop(0, n // BLOCK, solved, 0)
    r0, r1, r2, r3 = (w[...].reshape(3 * n, n) for w in (w0, w1, w2, w3))

    def schur(m, carry):
        l0, l1, l2, l3 = (wide_left(c[:, chunk(m)].T) for c in (c0, c1, c2, c3))
        corner[chunk(m), :] = product_wide(l0, r0) + product_wide(l3, r3)
        across[chunk(m), :] = product_wide(l0, r1) + product_wide(l3, r2)
        corner_far[chunk(m), :] = product_wide(l1, r1) + product_wide(l2, r2)
        return carry

    lax.fori_loop(0, n // BLOCK, schur, 0)
    own = wide_left(jnp.concatenate([b[0, :, :n], b[1, :, :n]], axis=0))
    far = wide_left(jnp.concatenate([b[2, :, :n], b[3, :, :n]], axis=0))
    half = 2 * slab
    near[:half, :] = -product_wide(own, r0)
    near[half:, :] = -product_wide(far, r3)
    away[:half, :] = -product_wide(own, r1)
    away[half:, :] = -product_wide(far, r2)
    for ref, siblings_of in ((near, (0, 3)), (away, (1, 2))):
        for s in siblings_of:
            rows = slice(s * slab, (s + 1) * slab)
            ref[rows, :] = ref[rows, :] + b[s, :, n:]


def middle(inv_own, inv_far, cp, b):
    n = inv_own.shape[0]
    count = b.shape[0] * b.shape[1]
    square = jax.ShapeDtypeStruct((n, n), jnp.float32)
    return pl.pallas_call(
        middle_kernel,
        out_shape=[jax.ShapeDtypeStruct((n, 2 * n), jnp.float32)]
        + [square] * 3
        + [jax.ShapeDtypeStruct((count, n), jnp.float32)] * 2,
        in_specs=[pl.BlockSpec(memory_space=pltpu.VMEM)] * 7,
        out_specs=[pl.BlockSpec(memory_space=pltpu.VMEM)] * 6,
        scratch_shapes=[pltpu.VMEM((3, n, n), jnp.bfloat16)] * 4,
        compiler_params=pltpu.CompilerParams(vmem_limit_bytes=48 * 1024 * 1024),
        cost_estimate=pl.CostEstimate(flops=2 * 10**10, bytes_accessed=10**7, transcendentals=0),
        name="middle",
    )(inv_own, inv_far, *cp, b)


def odd_kernel(half_ref, corner, across, corner_far, near, away, *refs):
    (own, partner, opposite, mate), (rhs_ref, mat_ref, row_ref) = refs[:4], refs[4:]
    n = corner.shape[0]
    h = n // 2
    order = 2 * n
    steps = order // BLOCK
    mat_ref[:n, :n] = -corner[...]
    mat_ref[:n, n:order] = -across[...]
    mat_ref[n:, :n] = -across[...].T
    mat_ref[n:, n:order] = -corner_far[...]
    for far, same, piece in ((0, 1, own), (0, 0, mate), (1, 1, opposite), (1, 0, partner)):
        side = half_ref[0] if same else 1 - half_ref[0]
        rows = slice(far * n, (far + 1) * n)
        cols = pl.ds(pl.multiple_of(far * n + side * h, h), h)
        mat_ref[rows, cols] = mat_ref[rows, cols] + piece[...]
    mat_ref[:n, order:] = near[...].T
    mat_ref[n:, order:] = away[...].T
    diag = mat_ref[:BLOCK, :BLOCK]
    for k in range(steps):
        ks = slice(k * BLOCK, (k + 1) * BLOCK)
        rest = slice((k + 1) * BLOCK, mat_ref.shape[1])
        (inverse,) = invert_blocks([diag], 64)
        row = product_wide(wide_left(inverse), wide_right(mat_ref[ks, rest]))
        row_ref[:, rest] = wide_right(row)
        if k + 1 < steps:
            nxt = slice((k + 1) * BLOCK, (k + 2) * BLOCK)
            diag = mat_ref[nxt, nxt] - product_wide(wide_left(mat_ref[nxt, ks]), row_ref[:, nxt])

        def update(m, carry):
            @pl.when(m != k)
            def _():
                ms = pl.ds(pl.multiple_of(m * BLOCK, BLOCK), BLOCK)
                col = wide_left(mat_ref[ms, ks])
                mat_ref[ms, rest] = mat_ref[ms, rest] - product_wide(col, row_ref[:, rest])

            return carry

        lax.fori_loop(0, steps, update, 0)
        mat_ref[ks, rest] = row
    rhs_ref[...] = mat_ref[:, order:]


def odd_solve(half, blocks, pieces):
    order = 2 * blocks[0].shape[0]
    count = blocks[3].shape[0]
    return pl.pallas_call(
        odd_kernel,
        out_shape=jax.ShapeDtypeStruct((order, count), jnp.float32),
        in_specs=[pl.BlockSpec(memory_space=pltpu.SMEM)]
        + [pl.BlockSpec(memory_space=pltpu.VMEM)] * 9,
        out_specs=pl.BlockSpec(memory_space=pltpu.VMEM),
        scratch_shapes=[
            pltpu.VMEM((order, order + count), jnp.float32),
            pltpu.VMEM((3 * BLOCK, order + count), jnp.bfloat16),
        ],
        compiler_params=pltpu.CompilerParams(vmem_limit_bytes=40 * 1024 * 1024),
        cost_estimate=pl.CostEstimate(flops=10**10, bytes_accessed=10**8, transcendentals=0),
        name="odd_solve",
    )(half, *blocks, *pieces)


def sibling(piece, x):
    return lax.ppermute(piece, "child", [(i, i ^ x) for i in range(4)])


def siblings(piece):
    return [piece] + [sibling(piece, x) for x in range(1, 4)]


def tiles(piece):
    count = lax.axis_size("tile")
    stack = jnp.broadcast_to(piece[None], (count,) + piece.shape)
    stack = lax.all_to_all(stack, "tile", 0, 0, tiled=False)
    return stack.reshape(count * piece.shape[0], piece.shape[1])


def by_relation(stack, pos):
    pick = [jnp.where(pos == 0, stack[i], 0.0) for i in range(4)]
    for x in range(1, 4):
        pick = [jnp.where(pos == x, stack[i ^ x], pick[i]) for i in range(4)]
    return jnp.stack(pick)


def on_device(children):
    own = children[0]
    n = own.shape[2] // 4
    h = n // 2
    slab = own.shape[1]
    pos = lax.axis_index("child")
    is_even = pos % 2 == 0

    def halves(piece, keep_first):
        keep = jnp.where(keep_first, piece[:, :h], piece[:, h:])
        give = jnp.where(keep_first, piece[:, h:], piece[:, :h])
        return keep, give

    ev_rows = jnp.where(is_even, own[0], own[1])
    od_rows = jnp.where(is_even, own[1], own[0])
    ev_diag = jnp.where(is_even, ev_rows[:, :n], ev_rows[:, n : 2 * n])
    od_diag = jnp.where(is_even, od_rows[:, n : 2 * n], od_rows[:, :n])
    couple = jnp.where(is_even, ev_rows[:, n : 2 * n], ev_rows[:, :n])
    points = own[2:, :, : 2 * n].reshape(2 * slab, 2 * n)
    points = jnp.where(is_even, points, jnp.concatenate([points[:, n:], points[:, :n]], axis=1))
    border = jnp.stack([ev_rows[:, 2 * n :], od_rows[:, 2 * n :]])
    ev_keep, ev_give = halves(ev_diag, is_even)
    od_keep, od_give = halves(od_diag, is_even)
    ev = ev_keep + lax.ppermute(ev_give, "child", [(i, i ^ 1) for i in range(4)])
    od = od_keep + lax.ppermute(od_give, "child", [(i, i ^ 3) for i in range(4)])
    ev, od = lax.optimization_barrier((ev, od))
    b = lax.all_gather(points, "child", axis=0, tiled=False)
    ev = tiles(ev)
    ev, couple, border = lax.optimization_barrier((ev, couple, border))
    border = lax.all_gather(border, "tile", axis=0, tiled=True)
    half = (pos % 2).astype(jnp.int32).reshape(1)
    partner = sibling(ev, 1)
    cp = tiles(couple)
    ev, partner = lax.optimization_barrier((ev, partner))
    opposite, mate = sibling(ev, 2), sibling(ev, 3)
    inv_own = even_inverse(half, ev, partner)
    inv_own, opposite, mate, cp, od = lax.optimization_barrier((inv_own, opposite, mate, cp, od))
    cp = siblings(cp)
    b = by_relation(b, pos)
    inv_far = even_inverse(half, opposite, mate)
    od = siblings(tiles(od))

    k_own, *blocks = middle(inv_own, inv_far, cp, b)
    wo = odd_solve(half, blocks, od)
    be_own = jnp.concatenate([b[0][:, :n], b[1][:, :n]], axis=0)
    we = product_high(inv_own, be_own.T)
    we = jnp.concatenate([we, jnp.zeros((n, 4 * slab), jnp.float32)], axis=1)
    we = we - product_high(k_own, wo)
    w = jnp.stack([we, wo[:n]]).reshape(2, n // slab, slab, 8 * slab).transpose(1, 0, 2, 3)
    prod = product_left_t(w.reshape(2 * n, 8 * slab), border.reshape(2 * n, 2 * n))
    prod = prod.reshape(4, 2, slab, 2 * n)
    own_map = own[2:, :, 2 * n :]
    res = jnp.concatenate([(own_map - prod[0])[None], -prod[1:]], axis=0)
    return by_relation(res, pos).reshape(4, 2, slab, 1, 2 * n)


def solution(mesh):
    in_specs = (P(("parent", "child"), None, "tile", None),)
    out_specs = P("parent", None, "tile", "child", None)
    return jax.shard_map(
        on_device, mesh=mesh, in_specs=in_specs, out_specs=out_specs, check_vma=False
    )
```

```python
import jax
import jax.numpy as jnp
from jax import lax
from jax.experimental import pallas as pl
from jax.experimental.pallas import tpu as pltpu
from jax.sharding import PartitionSpec as P

precise = lax.Precision.HIGHEST
BLOCK = 128
GROUP = 8


def product_high(left_mat, right_mat):
    return jnp.dot(left_mat, right_mat, precision=precise, preferred_element_type=jnp.float32)


def product_left_t(left_mat, right_mat, precision=lax.Precision.HIGH):
    return lax.dot_general(
        left_mat,
        right_mat,
        (((0,), (0,)), ((), ())),
        precision=precision,
        preferred_element_type=jnp.float32,
    )


def split(mat):
    high = mat.astype(jnp.bfloat16)
    return high, (mat - high.astype(jnp.float32)).astype(jnp.bfloat16)


def wide_left(mat):
    high, low = split(mat)
    return jnp.concatenate([high, low, high], axis=1)


def wide_right(mat):
    high, low = split(mat)
    return jnp.concatenate([high, high, low], axis=0)


def product_wide(left_wide, right_wide):
    return jnp.dot(left_wide, right_wide, preferred_element_type=jnp.float32)


def pivot_group(rows, g):
    shape = (GROUP, BLOCK)
    sub = lax.broadcasted_iota(jnp.int32, shape, 0)
    lane = lax.broadcasted_iota(jnp.int32, shape, 1)
    first = GROUP * g

    def row_of(v, j):
        return jnp.broadcast_to(v[j : j + 1, :], shape)

    def col_of(v, j):
        return jnp.broadcast_to(v[:, first + j : first + j + 1], shape)

    top = rows[g]
    cols = [col_of(top, j) for j in range(GROUP)]
    pivot = row_of(cols[0], 0)
    for j in range(GROUP):
        inverse = 1.0 / pivot
        if j + 1 < GROUP:
            ahead = cols[j] * row_of(cols[j + 1], j)
            pivot = row_of(cols[j + 1], j + 1) - row_of(ahead, j + 1) * inverse
        scaled = jnp.where(lane == first + j, inverse, row_of(top, j) * inverse)
        cleared = jnp.where(lane == first + j, 0.0, top)
        top = jnp.where(sub == j, scaled, cleared - cols[j] * scaled)
        for l in range(j + 1, GROUP):
            entry = row_of(cols[l], j)
            cols[l] = jnp.where(sub == j, entry * inverse, cols[l] - (cols[j] * entry) * inverse)
    spread = [row_of(top, j) for j in range(GROUP)]
    out = []
    for h, v in enumerate(rows):
        if h == g:
            out.append(top)
            continue
        terms = [col_of(v, j) * spread[j] for j in range(GROUP)]
        while len(terms) > 1:
            terms = [terms[i] + terms[i + 1] for i in range(0, len(terms), 2)]
        pivots = (lane >= first) & (lane < first + GROUP)
        out.append(jnp.where(pivots, 0.0, v) - terms[0])
    return out


def invert_blocks(mats, width, beside=None):
    count = BLOCK // GROUP
    inner = width // GROUP

    def body(p, carry):
        if beside is not None:
            beside(p)
        out = []
        for i in range(len(mats)):
            groups = list(carry[count * i : count * (i + 1)])
            panel = groups[:inner]
            for g in range(inner):
                panel = pivot_group(panel, g)
            panel = jnp.concatenate(panel, axis=0)
            rest = jnp.concatenate(groups[inner:], axis=0)
            update = product_high(rest[:, :width], panel)
            lanes = lax.broadcasted_iota(jnp.int32, rest.shape, 1)
            rest = jnp.where(lanes < width, 0.0, rest) - update
            turned = pltpu.roll(jnp.concatenate([rest, panel], axis=0), BLOCK - width, 1)
            out += [turned[GROUP * h : GROUP * (h + 1)] for h in range(count)]
        return tuple(out)

    init = tuple(m[GROUP * h : GROUP * (h + 1), :] for m in mats for h in range(count))
    res = lax.fori_loop(0, BLOCK // width, body, init)
    return [jnp.concatenate(res[count * i : count * (i + 1)], axis=0) for i in range(len(mats))]


def even_kernel(half_ref, mine_ref, other_ref, inv_ref):
    n = inv_ref.shape[0]
    h = n // 2
    mine = pl.ds(pl.multiple_of(half_ref[0] * h, h), h)
    other = pl.ds(pl.multiple_of((1 - half_ref[0]) * h, h), h)
    inv_ref[:, mine] = mine_ref[...]
    inv_ref[:, other] = other_ref[...]
    for k in range(n // BLOCK):
        ks = slice(k * BLOCK, (k + 1) * BLOCK)
        (diag,) = invert_blocks([inv_ref[ks, ks]], 64)
        inv_ref[ks, ks] = jnp.eye(BLOCK, dtype=jnp.float32)
        row = product_high(diag, inv_ref[ks, :])
        for m in range(n // BLOCK):
            if m != k:
                ms = slice(m * BLOCK, (m + 1) * BLOCK)
                col = inv_ref[ms, ks]
                inv_ref[ms, ks] = jnp.zeros((BLOCK, BLOCK), jnp.float32)
                inv_ref[ms, :] = inv_ref[ms, :] - product_high(col, row)
        inv_ref[ks, :] = row


def even_inverse(half, mine, other):
    n = mine.shape[0]
    return pl.pallas_call(
        even_kernel,
        out_shape=jax.ShapeDtypeStruct((n, n), jnp.float32),
        in_specs=[pl.BlockSpec(memory_space=pltpu.SMEM)]
        + [pl.BlockSpec(memory_space=pltpu.VMEM)] * 2,
        out_specs=pl.BlockSpec(memory_space=pltpu.VMEM),
        compiler_params=pltpu.CompilerParams(vmem_limit_bytes=40 * 1024 * 1024),
        cost_estimate=pl.CostEstimate(flops=10**10, bytes_accessed=10**8, transcendentals=0),
        name="even_inverse",
    )(half, mine, other)


def middle_kernel(
    inv_own, inv_far, c0, c1, c2, c3, b, k_own, corner, across, corner_far, near, away, w0, w1, w2, w3
):
    n = corner.shape[0]
    slab = b.shape[1]

    def chunk(m):
        return pl.ds(pl.multiple_of(m * BLOCK, BLOCK), BLOCK)

    for i, (inv, c, wide) in enumerate(
        ((inv_own, c0, w0), (inv_own, c1, w1), (inv_far, c3, w3), (inv_far, c2, w2))
    ):

        def solved(m, carry, i=i, inv=inv, c=c, wide=wide):
            rows = product_high(inv[chunk(m), :], c[...])
            if i < 2:
                k_own[chunk(m), i * n : (i + 1) * n] = rows
            high, low = split(rows)
            wide[0, chunk(m), :] = high
            wide[1, chunk(m), :] = high
            wide[2, chunk(m), :] = low
            return carry

        lax.fori_loop(0, n // BLOCK, solved, 0)
    r0, r1, r2, r3 = (w[...].reshape(3 * n, n) for w in (w0, w1, w2, w3))

    def schur(m, carry):
        l0, l1, l2, l3 = (wide_left(c[:, chunk(m)].T) for c in (c0, c1, c2, c3))
        corner[chunk(m), :] = product_wide(l0, r0) + product_wide(l3, r3)
        across[chunk(m), :] = product_wide(l0, r1) + product_wide(l3, r2)
        corner_far[chunk(m), :] = product_wide(l1, r1) + product_wide(l2, r2)
        return carry

    lax.fori_loop(0, n // BLOCK, schur, 0)
    own = wide_left(jnp.concatenate([b[0, :, :n], b[1, :, :n]], axis=0))
    far = wide_left(jnp.concatenate([b[2, :, :n], b[3, :, :n]], axis=0))
    half = 2 * slab
    near[:half, :] = -product_wide(own, r0)
    near[half:, :] = -product_wide(far, r3)
    away[:half, :] = -product_wide(own, r1)
    away[half:, :] = -product_wide(far, r2)
    for ref, siblings_of in ((near, (0, 3)), (away, (1, 2))):
        for s in siblings_of:
            rows = slice(s * slab, (s + 1) * slab)
            ref[rows, :] = ref[rows, :] + b[s, :, n:]


def middle(inv_own, inv_far, cp, b):
    n = inv_own.shape[0]
    count = b.shape[0] * b.shape[1]
    square = jax.ShapeDtypeStruct((n, n), jnp.float32)
    return pl.pallas_call(
        middle_kernel,
        out_shape=[jax.ShapeDtypeStruct((n, 2 * n), jnp.float32)]
        + [square] * 3
        + [jax.ShapeDtypeStruct((count, n), jnp.float32)] * 2,
        in_specs=[pl.BlockSpec(memory_space=pltpu.VMEM)] * 7,
        out_specs=[pl.BlockSpec(memory_space=pltpu.VMEM)] * 6,
        scratch_shapes=[pltpu.VMEM((3, n, n), jnp.bfloat16)] * 4,
        compiler_params=pltpu.CompilerParams(vmem_limit_bytes=48 * 1024 * 1024),
        cost_estimate=pl.CostEstimate(flops=2 * 10**10, bytes_accessed=10**7, transcendentals=0),
        name="middle",
    )(inv_own, inv_far, *cp, b)


def odd_kernel(half_ref, corner, across, corner_far, near, away, *refs):
    (own, partner, opposite, mate), (rhs_ref, mat_ref, row_ref) = refs[:4], refs[4:]
    n = corner.shape[0]
    h = n // 2
    order = 2 * n
    steps = order // BLOCK
    mat_ref[:n, :n] = -corner[...]
    mat_ref[:n, n:order] = -across[...]
    mat_ref[n:, :n] = -across[...].T
    mat_ref[n:, n:order] = -corner_far[...]
    for far, same, piece in ((0, 1, own), (0, 0, mate), (1, 1, opposite), (1, 0, partner)):
        side = half_ref[0] if same else 1 - half_ref[0]
        rows = slice(far * n, (far + 1) * n)
        cols = pl.ds(pl.multiple_of(far * n + side * h, h), h)
        mat_ref[rows, cols] = mat_ref[rows, cols] + piece[...]
    mat_ref[:n, order:] = near[...].T
    mat_ref[n:, order:] = away[...].T
    diag = mat_ref[:BLOCK, :BLOCK]
    def eliminate(k, m):
        ks = slice(k * BLOCK, (k + 1) * BLOCK)
        rest = slice((k + 1) * BLOCK, mat_ref.shape[1])
        ms = pl.ds(pl.multiple_of(m * BLOCK, BLOCK), BLOCK)
        col = wide_left(jnp.where(m == k, 0.0, mat_ref[ms, ks]))
        mat_ref[ms, rest] = mat_ref[ms, rest] - product_wide(col, row_ref[:, rest])

    width = BLOCK // 2
    share = steps * width // BLOCK
    for k in range(steps):
        ks = slice(k * BLOCK, (k + 1) * BLOCK)
        rest = slice((k + 1) * BLOCK, mat_ref.shape[1])

        def beside(p, k=k):
            for i in range(share):
                eliminate(k - 1, p * share + i)

        (inverse,) = invert_blocks([diag], width, beside if k else None)
        row = product_wide(wide_left(inverse), wide_right(mat_ref[ks, rest]))
        row_ref[:, rest] = wide_right(row)
        if k + 1 < steps:
            nxt = slice((k + 1) * BLOCK, (k + 2) * BLOCK)
            diag = mat_ref[nxt, nxt] - product_wide(wide_left(mat_ref[nxt, ks]), row_ref[:, nxt])
        mat_ref[ks, rest] = row

    def last(m, carry):
        eliminate(steps - 1, m)
        return carry

    lax.fori_loop(0, steps, last, 0)
    rhs_ref[...] = mat_ref[:, order:]


def odd_solve(half, blocks, pieces):
    order = 2 * blocks[0].shape[0]
    count = blocks[3].shape[0]
    return pl.pallas_call(
        odd_kernel,
        out_shape=jax.ShapeDtypeStruct((order, count), jnp.float32),
        in_specs=[pl.BlockSpec(memory_space=pltpu.SMEM)]
        + [pl.BlockSpec(memory_space=pltpu.VMEM)] * 9,
        out_specs=pl.BlockSpec(memory_space=pltpu.VMEM),
        scratch_shapes=[
            pltpu.VMEM((order, order + count), jnp.float32),
            pltpu.VMEM((3 * BLOCK, order + count), jnp.bfloat16),
        ],
        compiler_params=pltpu.CompilerParams(vmem_limit_bytes=40 * 1024 * 1024),
        cost_estimate=pl.CostEstimate(flops=10**10, bytes_accessed=10**8, transcendentals=0),
        name="odd_solve",
    )(half, *blocks, *pieces)


def sibling(piece, x):
    return lax.ppermute(piece, "child", [(i, i ^ x) for i in range(4)])


def siblings(piece):
    return [piece] + [sibling(piece, x) for x in range(1, 4)]


def tiles(piece):
    count = lax.axis_size("tile")
    stack = jnp.broadcast_to(piece[None], (count,) + piece.shape)
    stack = lax.all_to_all(stack, "tile", 0, 0, tiled=False)
    return stack.reshape(count * piece.shape[0], piece.shape[1])


def by_relation(stack, pos):
    pick = [jnp.where(pos == 0, stack[i], 0.0) for i in range(4)]
    for x in range(1, 4):
        pick = [jnp.where(pos == x, stack[i ^ x], pick[i]) for i in range(4)]
    return jnp.stack(pick)


def on_device(children):
    own = children[0]
    n = own.shape[2] // 4
    h = n // 2
    slab = own.shape[1]
    pos = lax.axis_index("child")
    is_even = pos % 2 == 0

    def halves(piece, keep_first):
        keep = jnp.where(keep_first, piece[:, :h], piece[:, h:])
        give = jnp.where(keep_first, piece[:, h:], piece[:, :h])
        return keep, give

    ev_rows = jnp.where(is_even, own[0], own[1])
    od_rows = jnp.where(is_even, own[1], own[0])
    ev_diag = jnp.where(is_even, ev_rows[:, :n], ev_rows[:, n : 2 * n])
    od_diag = jnp.where(is_even, od_rows[:, n : 2 * n], od_rows[:, :n])
    couple = jnp.where(is_even, ev_rows[:, n : 2 * n], ev_rows[:, :n])
    points = own[2:, :, : 2 * n].reshape(2 * slab, 2 * n)
    points = jnp.where(is_even, points, jnp.concatenate([points[:, n:], points[:, :n]], axis=1))
    border = jnp.stack([ev_rows[:, 2 * n :], od_rows[:, 2 * n :]])
    ev_keep, ev_give = halves(ev_diag, is_even)
    od_keep, od_give = halves(od_diag, is_even)
    ev = ev_keep + lax.ppermute(ev_give, "child", [(i, i ^ 1) for i in range(4)])
    od = od_keep + lax.ppermute(od_give, "child", [(i, i ^ 3) for i in range(4)])
    ev, od = lax.optimization_barrier((ev, od))
    b = lax.all_gather(points, "child", axis=0, tiled=False)
    ev = tiles(ev)
    ev, couple, border = lax.optimization_barrier((ev, couple, border))
    border = lax.all_gather(border, "tile", axis=0, tiled=True)
    half = (pos % 2).astype(jnp.int32).reshape(1)
    partner = sibling(ev, 1)
    cp = tiles(couple)
    ev, partner = lax.optimization_barrier((ev, partner))
    opposite, mate = sibling(ev, 2), sibling(ev, 3)
    inv_own = even_inverse(half, ev, partner)
    inv_own, opposite, mate, cp, od = lax.optimization_barrier((inv_own, opposite, mate, cp, od))
    cp = siblings(cp)
    b = by_relation(b, pos)
    inv_far = even_inverse(half, opposite, mate)
    od = siblings(tiles(od))

    k_own, *blocks = middle(inv_own, inv_far, cp, b)
    wo = odd_solve(half, blocks, od)
    be_own = jnp.concatenate([b[0][:, :n], b[1][:, :n]], axis=0)
    we = product_high(inv_own, be_own.T)
    we = jnp.concatenate([we, jnp.zeros((n, 4 * slab), jnp.float32)], axis=1)
    we = we - product_high(k_own, wo)
    w = jnp.stack([we, wo[:n]]).reshape(2, n // slab, slab, 8 * slab).transpose(1, 0, 2, 3)
    prod = product_left_t(w.reshape(2 * n, 8 * slab), border.reshape(2 * n, 2 * n))
    prod = prod.reshape(4, 2, slab, 2 * n)
    own_map = own[2:, :, 2 * n :]
    res = jnp.concatenate([(own_map - prod[0])[None], -prod[1:]], axis=0)
    return by_relation(res, pos).reshape(4, 2, slab, 1, 2 * n)


def solution(mesh):
    in_specs = (P(("parent", "child"), None, "tile", None),)
    out_specs = P("parent", None, "tile", "child", None)
    return jax.shard_map(
        on_device, mesh=mesh, in_specs=in_specs, out_specs=out_specs, check_vma=False
    )
```

```python
import jax
import jax.numpy as jnp
from jax import lax
from jax.experimental import pallas as pl
from jax.experimental.pallas import tpu as pltpu
from jax.sharding import PartitionSpec as P

precise = lax.Precision.HIGHEST
BLOCK = 128
GROUP = 8


def product_high(left_mat, right_mat):
    return jnp.dot(left_mat, right_mat, precision=precise, preferred_element_type=jnp.float32)


def product_left_t(left_mat, right_mat, precision=lax.Precision.HIGH):
    return lax.dot_general(
        left_mat,
        right_mat,
        (((0,), (0,)), ((), ())),
        precision=precision,
        preferred_element_type=jnp.float32,
    )


def split(mat):
    high = mat.astype(jnp.bfloat16)
    return high, (mat - high.astype(jnp.float32)).astype(jnp.bfloat16)


def wide_left(mat):
    high, low = split(mat)
    return jnp.concatenate([high, low, high], axis=1)


def wide_right(mat):
    high, low = split(mat)
    return jnp.concatenate([high, high, low], axis=0)


def product_wide(left_wide, right_wide):
    return jnp.dot(left_wide, right_wide, preferred_element_type=jnp.float32)


def pivot_group(rows, g):
    shape = (GROUP, BLOCK)
    sub = lax.broadcasted_iota(jnp.int32, shape, 0)
    lane = lax.broadcasted_iota(jnp.int32, shape, 1)
    first = GROUP * g

    def row_of(v, j):
        return jnp.broadcast_to(v[j : j + 1, :], shape)

    def col_of(v, j):
        return jnp.broadcast_to(v[:, first + j : first + j + 1], shape)

    top = rows[g]
    cols = [col_of(top, j) for j in range(GROUP)]
    pivot = row_of(cols[0], 0)
    for j in range(GROUP):
        inverse = 1.0 / pivot
        if j + 1 < GROUP:
            ahead = cols[j] * row_of(cols[j + 1], j)
            pivot = row_of(cols[j + 1], j + 1) - row_of(ahead, j + 1) * inverse
        scaled = jnp.where(lane == first + j, inverse, row_of(top, j) * inverse)
        cleared = jnp.where(lane == first + j, 0.0, top)
        top = jnp.where(sub == j, scaled, cleared - cols[j] * scaled)
        for l in range(j + 1, GROUP):
            entry = row_of(cols[l], j)
            cols[l] = jnp.where(sub == j, entry * inverse, cols[l] - (cols[j] * entry) * inverse)
    spread = [row_of(top, j) for j in range(GROUP)]
    out = []
    for h, v in enumerate(rows):
        if h == g:
            out.append(top)
            continue
        terms = [col_of(v, j) * spread[j] for j in range(GROUP)]
        while len(terms) > 1:
            terms = [terms[i] + terms[i + 1] for i in range(0, len(terms), 2)]
        pivots = (lane >= first) & (lane < first + GROUP)
        out.append(jnp.where(pivots, 0.0, v) - terms[0])
    return out


def invert_blocks(mats, width, beside=None):
    count = BLOCK // GROUP
    inner = width // GROUP

    def body(p, carry):
        if beside is not None:
            beside(p)
        out = []
        for i in range(len(mats)):
            groups = list(carry[count * i : count * (i + 1)])
            panel = groups[:inner]
            for g in range(inner):
                panel = pivot_group(panel, g)
            panel = jnp.concatenate(panel, axis=0)
            rest = jnp.concatenate(groups[inner:], axis=0)
            update = product_high(rest[:, :width], panel)
            lanes = lax.broadcasted_iota(jnp.int32, rest.shape, 1)
            rest = jnp.where(lanes < width, 0.0, rest) - update
            turned = pltpu.roll(jnp.concatenate([rest, panel], axis=0), BLOCK - width, 1)
            out += [turned[GROUP * h : GROUP * (h + 1)] for h in range(count)]
        return tuple(out)

    init = tuple(m[GROUP * h : GROUP * (h + 1), :] for m in mats for h in range(count))
    res = lax.fori_loop(0, BLOCK // width, body, init)
    return [jnp.concatenate(res[count * i : count * (i + 1)], axis=0) for i in range(len(mats))]


def even_kernel(half_ref, mine_ref, other_ref, inv_ref):
    n = inv_ref.shape[0]
    h = n // 2
    mine = pl.ds(pl.multiple_of(half_ref[0] * h, h), h)
    other = pl.ds(pl.multiple_of((1 - half_ref[0]) * h, h), h)
    inv_ref[:, mine] = mine_ref[...]
    inv_ref[:, other] = other_ref[...]
    for k in range(n // BLOCK):
        ks = slice(k * BLOCK, (k + 1) * BLOCK)
        (diag,) = invert_blocks([inv_ref[ks, ks]], 64)
        inv_ref[ks, ks] = jnp.eye(BLOCK, dtype=jnp.float32)
        row = product_high(diag, inv_ref[ks, :])
        for m in range(n // BLOCK):
            if m != k:
                ms = slice(m * BLOCK, (m + 1) * BLOCK)
                col = inv_ref[ms, ks]
                inv_ref[ms, ks] = jnp.zeros((BLOCK, BLOCK), jnp.float32)
                inv_ref[ms, :] = inv_ref[ms, :] - product_high(col, row)
        inv_ref[ks, :] = row


def even_inverse(half, mine, other):
    n = mine.shape[0]
    return pl.pallas_call(
        even_kernel,
        out_shape=jax.ShapeDtypeStruct((n, n), jnp.float32),
        in_specs=[pl.BlockSpec(memory_space=pltpu.SMEM)]
        + [pl.BlockSpec(memory_space=pltpu.VMEM)] * 2,
        out_specs=pl.BlockSpec(memory_space=pltpu.VMEM),
        compiler_params=pltpu.CompilerParams(vmem_limit_bytes=40 * 1024 * 1024),
        cost_estimate=pl.CostEstimate(flops=10**10, bytes_accessed=10**8, transcendentals=0),
        name="even_inverse",
    )(half, mine, other)


def middle_kernel(pos_ref, inv_own, inv_far, c0, c1, c2, c3, b_ref, *refs):
    k_own, corner, across, corner_far, near, away, reach, w0, w1, w2, w3 = refs
    b = [b_ref[jnp.bitwise_xor(pos_ref[0], s)] for s in range(4)]
    n = corner.shape[0]
    slab = b_ref.shape[1]

    def chunk(m):
        return pl.ds(pl.multiple_of(m * BLOCK, BLOCK), BLOCK)

    for i, (inv, c, wide) in enumerate(
        ((inv_own, c0, w0), (inv_own, c1, w1), (inv_far, c3, w3), (inv_far, c2, w2))
    ):

        def solved(m, carry, i=i, inv=inv, c=c, wide=wide):
            rows = product_high(inv[chunk(m), :], c[...])
            if i < 2:
                k_own[chunk(m), i * n : (i + 1) * n] = rows
            high, low = split(rows)
            wide[0, chunk(m), :] = high
            wide[1, chunk(m), :] = high
            wide[2, chunk(m), :] = low
            return carry

        lax.fori_loop(0, n // BLOCK, solved, 0)
    r0, r1, r2, r3 = (w[...].reshape(3 * n, n) for w in (w0, w1, w2, w3))

    def schur(m, carry):
        l0, l1, l2, l3 = (wide_left(c[:, chunk(m)].T) for c in (c0, c1, c2, c3))
        corner[chunk(m), :] = product_wide(l0, r0) + product_wide(l3, r3)
        across[chunk(m), :] = product_wide(l0, r1) + product_wide(l3, r2)
        corner_far[chunk(m), :] = product_wide(l1, r1) + product_wide(l2, r2)
        return carry

    lax.fori_loop(0, n // BLOCK, schur, 0)
    be_own = jnp.concatenate([b[0][:, :n], b[1][:, :n]], axis=0)
    own = wide_left(be_own)
    far = wide_left(jnp.concatenate([b[2][:, :n], b[3][:, :n]], axis=0))
    reach[...] = product_high(inv_own[...], be_own.T)
    half = 2 * slab
    near[:half, :] = -product_wide(own, r0)
    near[half:, :] = -product_wide(far, r3)
    away[:half, :] = -product_wide(own, r1)
    away[half:, :] = -product_wide(far, r2)
    for ref, siblings_of in ((near, (0, 3)), (away, (1, 2))):
        for s in siblings_of:
            rows = slice(s * slab, (s + 1) * slab)
            ref[rows, :] = ref[rows, :] + b[s][:, n:]


def middle(pos, inv_own, inv_far, cp, b):
    n = inv_own.shape[0]
    count = b.shape[0] * b.shape[1]
    square = jax.ShapeDtypeStruct((n, n), jnp.float32)
    return pl.pallas_call(
        middle_kernel,
        out_shape=[jax.ShapeDtypeStruct((n, 2 * n), jnp.float32)]
        + [square] * 3
        + [jax.ShapeDtypeStruct((count, n), jnp.float32)] * 2
        + [jax.ShapeDtypeStruct((n, count // 2), jnp.float32)],
        in_specs=[pl.BlockSpec(memory_space=pltpu.SMEM)]
        + [pl.BlockSpec(memory_space=pltpu.VMEM)] * 7,
        out_specs=[pl.BlockSpec(memory_space=pltpu.VMEM)] * 7,
        scratch_shapes=[pltpu.VMEM((3, n, n), jnp.bfloat16)] * 4,
        compiler_params=pltpu.CompilerParams(vmem_limit_bytes=48 * 1024 * 1024),
        cost_estimate=pl.CostEstimate(flops=2 * 10**10, bytes_accessed=10**7, transcendentals=0),
        name="middle",
    )(pos, inv_own, inv_far, *cp, b)


def odd_kernel(half_ref, corner, across, corner_far, near, away, *refs):
    (own, partner, opposite, mate), (rhs_ref, mat_ref, row_ref) = refs[:4], refs[4:]
    n = corner.shape[0]
    h = n // 2
    order = 2 * n
    steps = order // BLOCK
    mat_ref[:n, :n] = -corner[...]
    mat_ref[:n, n:order] = -across[...]
    mat_ref[n:, :n] = -across[...].T
    mat_ref[n:, n:order] = -corner_far[...]
    for far, same, piece in ((0, 1, own), (0, 0, mate), (1, 1, opposite), (1, 0, partner)):
        side = half_ref[0] if same else 1 - half_ref[0]
        rows = slice(far * n, (far + 1) * n)
        cols = pl.ds(pl.multiple_of(far * n + side * h, h), h)
        mat_ref[rows, cols] = mat_ref[rows, cols] + piece[...]
    mat_ref[:n, order:] = near[...].T
    mat_ref[n:, order:] = away[...].T
    diag = mat_ref[:BLOCK, :BLOCK]
    def eliminate(k, m):
        ks = slice(k * BLOCK, (k + 1) * BLOCK)
        rest = slice((k + 1) * BLOCK, mat_ref.shape[1])
        ms = pl.ds(pl.multiple_of(m * BLOCK, BLOCK), BLOCK)
        col = wide_left(jnp.where(m == k, 0.0, mat_ref[ms, ks]))
        mat_ref[ms, rest] = mat_ref[ms, rest] - product_wide(col, row_ref[:, rest])

    width = BLOCK // 2
    share = steps * width // BLOCK
    for k in range(steps):
        ks = slice(k * BLOCK, (k + 1) * BLOCK)
        rest = slice((k + 1) * BLOCK, mat_ref.shape[1])

        def beside(p, k=k):
            for i in range(share):
                eliminate(k - 1, p * share + i)

        (inverse,) = invert_blocks([diag], width, beside if k else None)
        row = product_wide(wide_left(inverse), wide_right(mat_ref[ks, rest]))
        row_ref[:, rest] = wide_right(row)
        if k + 1 < steps:
            nxt = slice((k + 1) * BLOCK, (k + 2) * BLOCK)
            diag = mat_ref[nxt, nxt] - product_wide(wide_left(mat_ref[nxt, ks]), row_ref[:, nxt])
        mat_ref[ks, rest] = row

    def last(m, carry):
        eliminate(steps - 1, m)
        return carry

    lax.fori_loop(0, steps, last, 0)
    rhs_ref[...] = mat_ref[:, order:]


def odd_solve(half, blocks, pieces):
    order = 2 * blocks[0].shape[0]
    count = blocks[3].shape[0]
    return pl.pallas_call(
        odd_kernel,
        out_shape=jax.ShapeDtypeStruct((order, count), jnp.float32),
        in_specs=[pl.BlockSpec(memory_space=pltpu.SMEM)]
        + [pl.BlockSpec(memory_space=pltpu.VMEM)] * 9,
        out_specs=pl.BlockSpec(memory_space=pltpu.VMEM),
        scratch_shapes=[
            pltpu.VMEM((order, order + count), jnp.float32),
            pltpu.VMEM((3 * BLOCK, order + count), jnp.bfloat16),
        ],
        compiler_params=pltpu.CompilerParams(vmem_limit_bytes=40 * 1024 * 1024),
        cost_estimate=pl.CostEstimate(flops=10**10, bytes_accessed=10**8, transcendentals=0),
        name="odd_solve",
    )(half, *blocks, *pieces)


def sibling(piece, x):
    return lax.ppermute(piece, "child", [(i, i ^ x) for i in range(4)])


def siblings(piece):
    return [piece] + [sibling(piece, x) for x in range(1, 4)]


def tiles(piece):
    count = lax.axis_size("tile")
    stack = jnp.broadcast_to(piece[None], (count,) + piece.shape)
    stack = lax.all_to_all(stack, "tile", 0, 0, tiled=False)
    return stack.reshape(count * piece.shape[0], piece.shape[1])


def by_relation(stack, pos):
    pick = [jnp.where(pos == 0, stack[i], 0.0) for i in range(4)]
    for x in range(1, 4):
        pick = [jnp.where(pos == x, stack[i ^ x], pick[i]) for i in range(4)]
    return jnp.stack(pick)


def on_device(children):
    own = children[0]
    n = own.shape[2] // 4
    h = n // 2
    slab = own.shape[1]
    pos = lax.axis_index("child")
    is_even = pos % 2 == 0

    def halves(piece, keep_first):
        keep = jnp.where(keep_first, piece[:, :h], piece[:, h:])
        give = jnp.where(keep_first, piece[:, h:], piece[:, :h])
        return keep, give

    ev_rows = jnp.where(is_even, own[0], own[1])
    od_rows = jnp.where(is_even, own[1], own[0])
    ev_diag = jnp.where(is_even, ev_rows[:, :n], ev_rows[:, n : 2 * n])
    od_diag = jnp.where(is_even, od_rows[:, n : 2 * n], od_rows[:, :n])
    couple = jnp.where(is_even, ev_rows[:, n : 2 * n], ev_rows[:, :n])
    points = own[2:, :, : 2 * n].reshape(2 * slab, 2 * n)
    points = jnp.where(is_even, points, jnp.concatenate([points[:, n:], points[:, :n]], axis=1))
    border = jnp.stack([ev_rows[:, 2 * n :], od_rows[:, 2 * n :]])
    ev_keep, ev_give = halves(ev_diag, is_even)
    od_keep, od_give = halves(od_diag, is_even)
    ev = ev_keep + lax.ppermute(ev_give, "child", [(i, i ^ 1) for i in range(4)])
    od = od_keep + lax.ppermute(od_give, "child", [(i, i ^ 3) for i in range(4)])
    ev, od = lax.optimization_barrier((ev, od))
    b = lax.all_gather(points, "child", axis=0, tiled=False)
    ev = tiles(ev)
    ev, couple, border = lax.optimization_barrier((ev, couple, border))
    border = lax.all_gather(border, "tile", axis=0, tiled=True)
    half = (pos % 2).astype(jnp.int32).reshape(1)
    partner = sibling(ev, 1)
    cp = tiles(couple)
    ev, partner = lax.optimization_barrier((ev, partner))
    opposite, mate = sibling(ev, 2), sibling(ev, 3)
    inv_own = even_inverse(half, ev, partner)
    inv_own, opposite, mate, cp, od = lax.optimization_barrier((inv_own, opposite, mate, cp, od))
    cp = siblings(cp)
    inv_far = even_inverse(half, opposite, mate)
    od = siblings(tiles(od))

    k_own, *blocks, we = middle(pos.astype(jnp.int32).reshape(1), inv_own, inv_far, cp, b)
    wo = odd_solve(half, blocks, od)
    we = jnp.concatenate([we, jnp.zeros((n, 4 * slab), jnp.float32)], axis=1)
    we = we - product_high(k_own, wo)
    w = jnp.stack([we, wo[:n]]).reshape(2, n // slab, slab, 8 * slab).transpose(1, 0, 2, 3)
    prod = product_left_t(w.reshape(2 * n, 8 * slab), border.reshape(2 * n, 2 * n))
    prod = prod.reshape(4, 2, slab, 2 * n)
    own_map = own[2:, :, 2 * n :]
    res = jnp.concatenate([(own_map - prod[0])[None], -prod[1:]], axis=0)
    return by_relation(res, pos).reshape(4, 2, slab, 1, 2 * n)


def solution(mesh):
    in_specs = (P(("parent", "child"), None, "tile", None),)
    out_specs = P("parent", None, "tile", "child", None)
    return jax.shard_map(
        on_device, mesh=mesh, in_specs=in_specs, out_specs=out_specs, check_vma=False
    )
```
